32 devices in a mesh: rows: 8 (over y, x, core), vecs: 4 (over z).
Axes of the slice: x: 2, y: 2, z: 4, core: 2. Of those that a mesh axis runs over, the one named last changes fastest.
Arguments:
- eigvecs: bfloat16 [8192, 1024], P('rows', 'vecs'), may hold values from -6 to 6
- reflectors: bfloat16 [2, 8192, 1024], P(None, 'rows', 'vecs'), may hold values from -0.125 to 0.125
- factors: bfloat16 [2, 1024, 1024], replicated, as said below
Outputs:
- back_vecs: bfloat16 [8192, 1024], P('rows', 'vecs')
The draws below stay inside these ranges and needn't reach their ends.
Inputs may be any that keep to these rules, and one draw needn't show every extreme that they name: `factors`: each factor is upper triangular, its diagonal between 0.15 and 0.35.
All inputs are finite; a program needn't handle non-finite values.
Results may differ from the reference program's by a relative error of at most 0.01.
Values may be sent and summed in bfloat16 or wider, within the bound.
No kernel may reach another device: no remote copies, remote signals or barrier semaphores. Data moves between devices by JAX's collectives and lax.ppermute only.
A program may use at most 64 MiB of HBM per device.

```python
import jax
import jax.numpy as jnp
from jax import lax

NB = 1024
M = 8192
K = 1024


def draw_factors(key, part):
    first, second = jax.random.split(jax.random.fold_in(key, 7))
    diagon = jax.random.uniform(first, (2, NB), jnp.float32, 0.15, 0.35)
    offdiag = jax.random.normal(second, (2, NB, NB), jnp.float32) * (0.3 / NB ** 0.5)
    upper = jnp.triu(offdiag, 1) + diagon[:, :, None] * jnp.eye(NB, dtype=jnp.float32)[None]
    return upper.astype(jnp.bfloat16)


def steps_of(stream_key, shape, cuts, low, high):
    def one(axis_at, shards_of):
        steps = jax.random.uniform(jax.random.fold_in(jax.random.fold_in(stream_key, 6), axis_at), (shards_of,), jnp.float32, low / len(cuts), high / len(cuts))
        return jnp.repeat(jnp.exp(steps), shape[axis_at] // shards_of).reshape((-1,) + (1,) * (len(shape) - axis_at - 1))

    factor_of = one(*cuts[0])
    for cut in cuts[1:]:
        factor_of = factor_of * one(*cut)
    return factor_of


def normal_values(key, extent, scale, bound, pieces=(), held_as=jnp.bfloat16):
    array = jax.random.normal(key, extent, jnp.float32) * scale
    if len(pieces) > 0:
        array = steps_of(key, extent, pieces, -0.22, 0.18) * array
    return jnp.clip(array, min=-bound, max=bound).astype(held_as)


def setup_inputs(seed: int = 0) -> dict:
    streams_of = jax.random.split(jax.random.key(seed), 4)
    return {
        "eigvecs": normal_values(streams_of[0], (M, K), 1.0, 6.0, ((0, 8), (1, 4))),
        "reflectors": normal_values(streams_of[1], (2, M, NB), (2 * NB) ** -0.5, 0.125, ((1, 8), (2, 4))),
        "factors": draw_factors(jax.random.fold_in(streams_of[3], 71), 0),
    }


def reference(eigvecs, reflectors, factors):
    current = eigvecs
    for which in (1, 0):
        panel = reflectors[which]
        coeff = lax.dot_general(panel, current, (((0,), (0,)), ((), ())), preferred_element_type=jnp.float32).astype(jnp.bfloat16)
        scaled = jnp.dot(factors[which], coeff, preferred_element_type=jnp.float32).astype(jnp.bfloat16)
        update = jnp.dot(panel, scaled, preferred_element_type=jnp.float32)
        current = (current.astype(jnp.float32) - update).astype(jnp.bfloat16)
    return current
```

```python
import functools

import jax
import jax.numpy as jnp
from jax import lax
from jax.experimental import pallas as pl
from jax.experimental.pallas import tpu as pltpu
from jax.sharding import PartitionSpec as P

F32, BF16 = jnp.float32, jnp.bfloat16


def after(x, *others):
    return lax.optimization_barrier((x,) + others)[0]


def dot0(a, b):
    return lax.dot_general(a, b, (((0,), (0,)), ((), ())), preferred_element_type=F32)


def swap(x, bit, m):
    return lax.ppermute(x, "rows", [(i, i ^ bit) for i in range(m)])


def sum_rows(part, wide, m):
    odd = lax.axis_index("rows") % 2
    part = part.astype(BF16).reshape(-1, 2, wide // 2, part.shape[1])
    mine = lax.dynamic_index_in_dim(part, odd, 1, keepdims=False)
    other = lax.dynamic_index_in_dim(part, 1 - odd, 1, keepdims=False)
    mine = (mine.astype(F32) + swap(other, 1, m).astype(F32)).astype(BF16)
    bit = 2
    while bit < m:
        steps = [s * bit for s in range(1, 4) if s * bit < m]
        got = [swap(mine, s, m) for s in steps]
        mine = sum([g.astype(F32) for g in got], mine.astype(F32)).astype(BF16)
        bit *= 4
    return mine, swap(mine, 1, m)


def update_kernel(halves, pieces, wide, at_ref, factor_ref, current_ref, *refs):
    coeff_refs, panel_refs = refs[:halves], refs[halves : halves + pieces]
    out_ref, coeff, scaled = refs[halves + pieces :]

    @pl.when(pl.program_id(0) == 0)
    def _():
        at = 0
        for ref in coeff_refs:
            for k in range(ref.shape[0]):
                h = ref.shape[1]
                coeff[pl.ds(pl.multiple_of(at_ref[at], h), h), :] = ref[k]
                at += 1
        scaled[...] = jnp.dot(factor_ref[...], coeff[...], preferred_element_type=F32).astype(BF16)

    total = current_ref[...].astype(F32)
    first = sum(ref.shape[0] for ref in coeff_refs)
    update = None
    for k, ref in enumerate(panel_refs):
        rows = pl.ds(pl.multiple_of(at_ref[first + k], wide), wide)
        term = jnp.dot(ref[...], scaled[rows, :], preferred_element_type=F32)
        update = term if update is None else update + term
    out_ref[...] = (total - update).astype(BF16)


def update(current, factor, coeffs, panels, where):
    rows, columns = current.shape
    size, wide = factor.shape[0], panels[0].shape[1]
    tile = min(rows, 256)
    whole = lambda shape: pl.BlockSpec(shape, lambda i, at: (0,) * len(shape))
    grid_spec = pltpu.PrefetchScalarGridSpec(
        num_scalar_prefetch=1,
        grid=(rows // tile,),
        in_specs=[whole(factor.shape), pl.BlockSpec((tile, columns), lambda i, at: (i, 0))]
        + [whole(c.shape) for c in coeffs]
        + [pl.BlockSpec((tile, wide), lambda i, at: (i, 0)) for _ in panels],
        out_specs=pl.BlockSpec((tile, columns), lambda i, at: (i, 0)),
        scratch_shapes=[pltpu.VMEM((size, columns), BF16), pltpu.VMEM((size, columns), BF16)],
    )
    flops = 2 * size * columns * (size + rows)
    return pl.pallas_call(
        functools.partial(update_kernel, len(coeffs), len(panels), wide),
        grid_spec=grid_spec,
        out_shape=jax.ShapeDtypeStruct(current.shape, BF16),
        compiler_params=pltpu.CompilerParams(vmem_limit_bytes=32 << 20),
        cost_estimate=pl.CostEstimate(flops=flops, bytes_accessed=2 * size * (size + 2 * rows), transcendentals=0),
    )(where, factor, current, *coeffs, *panels)


class Line:
    def __init__(self, n):
        self.n = n
        self.me = lax.axis_index("vecs")

    def pairs(self, s, parity):
        out = []
        for i in range(parity, self.n - 1, 2):
            if i - s + 1 >= 0:
                out.append((i, i + 1))
            if i + s < self.n:
                out.append((i + 1, i))
        return out

    def send(self, x, pairs):
        return lax.ppermute(x, "vecs", pairs) if pairs else None

    def index(self, s, parity):
        return jnp.where(self.me % 2 == parity, self.me + s, self.me - s)


def body(n, m, eigvecs, reflectors, factors):
    line = Line(n)
    me = line.me
    wide = reflectors.shape[2]
    p1, p0 = reflectors[1], reflectors[0]
    current = eigvecs

    def gather(panel, gate_even, gate_odd):
        even, odd = {}, {}
        for s in range(1, n):
            from_e = panel if s == 1 else odd[s - 1]
            from_o = panel if s == 1 else even[s - 1]
            even[s] = line.send(gate_even(s, from_e), line.pairs(s, 0)) if from_e is not None else None
            odd[s] = line.send(gate_odd(s, from_o), line.pairs(s, 1)) if from_o is not None else None
        return even, odd

    keep = lambda s, x: x
    even1, odd1 = gather(p1, keep, keep)
    last = max(s for s in even1 if even1[s] is not None)
    e_gate = lambda s, x: after(x, even1[last]) if s == 1 else x
    o_gate = lambda s, x: after(x, even1[last - 1], odd1[last - 1]) if s == 1 else x
    even0, odd0 = gather(p0, e_gate, o_gate)

    def slots(panel, even, odd):
        out = [(me, [panel])]
        if n > 1:
            out.append((line.index(1, 0), [even[1]]))
        for s in range(1, n - 1):
            c = n - s - 1 if s % 2 else n - s + 1
            i, j = line.index(s, 1), line.index(c, 0)
            there = (i >= 0) & (i < n)
            out.append((jnp.where(there, i, j), [x for x in (odd[s], even[c]) if x is not None]))
        return out

    half = lax.axis_index("rows") % 2 * (wide // 2)
    for p, panel, even, odd in ((1, p1, even1, odd1), (0, p0, even0, odd0)):
        blocks = slots(panel, even, odd)
        groups = [blocks[:2]] + [[b] for b in blocks[2:]] if p == 1 else [blocks[:3]] + [[b] for b in blocks[3:]]
        coeffs, where, pieces, meets = [], [], [], []
        for group in groups:
            part = jnp.concatenate([sum(dot0(x, current) for x in xs) for _, xs in group], 0)
            coeffs += sum_rows(part, wide, m)
            where += [i * wide + half for i, _ in group] + [i * wide + wide // 2 - half for i, _ in group]
            for i, xs in group:
                pieces += xs
                meets += [i * wide for _ in xs]
        current = update(current, factors[p], coeffs, pieces, jnp.stack(where + meets).astype(jnp.int32))
    return current


def solution(mesh):
    n, m = mesh.shape["vecs"], mesh.shape["rows"]
    in_specs = (P("rows", "vecs"), P(None, "rows", "vecs"), P())
    out_specs = P("rows", "vecs")
    return jax.shard_map(
        functools.partial(body, n, m), mesh=mesh, in_specs=in_specs, out_specs=out_specs, check_vma=False
    )
```

```python
import functools

import jax
import jax.numpy as jnp
from jax import lax
from jax.experimental import pallas as pl
from jax.experimental.pallas import tpu as pltpu
from jax.sharding import PartitionSpec as P

F32, BF16 = jnp.float32, jnp.bfloat16
VMEM = 16 << 20
ANY = pl.BlockSpec(memory_space=pl.ANY)
IN_VMEM = pl.BlockSpec(memory_space=pltpu.VMEM)


def after(x, *others):
    return lax.optimization_barrier((x,) + others)[0]


def held(*xs):
    return [x for x in xs if x is not None]


def dot(a, b, ca, cb):
    return lax.dot_general(a, b, (((ca,), (cb,)), ((), ())), preferred_element_type=F32)


def swap(x, bit, m):
    return lax.ppermute(x, "rows", [(i, i ^ bit) for i in range(m)])


def sum_rows(mine, other, m, late=()):
    mine = (mine.astype(F32) + swap(other, 1, m).astype(F32)).astype(BF16)
    bit = 2
    while bit < m:
        got = [swap(mine, s * bit, m) for s in range(1, 4) if s * bit < m]
        mine = sum([after(g, *late).astype(F32) for g in got], mine.astype(F32)).astype(BF16)
        bit *= 4
    return mine, swap(mine, 1, m)


class Part:
    def __init__(self, arrays, blocks, here=None):
        self.arrays, self.blocks, self.here = arrays, blocks, here
        self.count, self.width = len(arrays), arrays[0].shape[1]


def start_parts(parts, refs, panels, sems):
    waits, at, column = [], 0, 0
    for k, part in enumerate(parts):
        place = panels.at[:, pl.ds(column, part.width)]
        copies = [pltpu.make_async_copy(ref, place, sems.at[k]) for ref in refs[at : at + part.count]]
        if part.count == 1:
            copies[0].start()
        else:
            here = part.here(lax.axis_index("vecs"))
            pl.when(here)(copies[0].start)
            pl.when(jnp.logical_not(here))(copies[1].start)
        waits.append(copies[0].wait)
        at += part.count
        column += part.width
    return waits


def coeff_kernel(parts, current_ref, *refs):
    n = sum(part.count for part in parts)
    mine_ref, other_ref, current, panels, sems = refs[n:]
    copy = pltpu.make_async_copy(current_ref, current, sems.at[len(parts)])
    copy.start()
    waits = start_parts(parts, refs[:n], panels, sems)
    copy.wait()
    half = current.shape[0] // 2
    odd = lax.axis_index("rows") % 2 == 1
    column = 0
    for part, wait in zip(parts, waits):
        wait()
        at = slice(column, column + part.width)
        total = dot(current[...], panels[:, at], 1, 0)
        mine_ref[:, at] = jnp.where(odd, total[half:], total[:half]).astype(BF16)
        other_ref[:, at] = jnp.where(odd, total[:half], total[half:]).astype(BF16)
        column += part.width


def update_kernel(p, last, groups, parts, factors_ref, current_ref, *refs):
    n = sum(part.count for part in parts)
    coeff_refs, panel_refs = refs[: 2 * len(groups)], refs[2 * len(groups) : 2 * len(groups) + n]
    out_ref, factor, coeff, scaled, met, current, panels, sems, panel_sems = refs[2 * len(groups) + n :]
    size, half = factor.shape[0], coeff.shape[0] // 2
    r, z = lax.axis_index("rows"), lax.axis_index("vecs")
    copies = []

    def copy(source, target):
        copies.append(pltpu.make_async_copy(source, target, sems.at[len(copies)]))
        copies[-1].start()
        return copies[-1]

    def columns(place, width):
        return pl.ds(pl.multiple_of(place(z), width), width)

    here = copy(current_ref, current)
    first = []
    for k, ref in enumerate(coeff_refs):
        rows = pl.ds(pl.multiple_of(jnp.where(r % 2 == k % 2, 0, half), half), half)
        at = 0
        for part in groups[k // 2]:
            for place, offset, width in part.blocks:
                first.append(copy(ref.at[:, pl.ds(at + offset, width)], coeff.at[rows, columns(place, width)]))
            at += part.width
    tiles = []
    for t in reversed(range(0, size, 256)):
        rows, cols = pl.ds(t, 256), pl.ds(t, size - t)
        tiles.append((t, copy(factors_ref.at[p, rows, cols], factor.at[rows, cols])))
    waits = start_parts(parts, panel_refs, panels, panel_sems)
    here.wait()
    start = current[...].astype(F32)
    if last:
        start = start.T
    for c in first:
        c.wait()
    for t, c in tiles:
        c.wait()
        scaled[:, t : t + 256] = dot(coeff[:, t:], factor[t : t + 256, t:], 1, 1).astype(BF16)
    at = 0
    for part in parts:
        for place, offset, width in part.blocks:
            met[:, at + offset : at + offset + width] = scaled[:, columns(place, width)]
        at += part.width
    for wait in waits:
        wait()
    total = dot(panels[...], met[...], 1, 1) if last else dot(met[...], panels[...], 1, 1)
    out_ref[...] = (start - total).astype(BF16)


def coeff(current, parts):
    columns, rows = current.shape
    size = sum(part.width for part in parts)
    arrays = [x for part in parts for x in part.arrays]
    return pl.pallas_call(
        functools.partial(coeff_kernel, parts),
        in_specs=[ANY] * (1 + len(arrays)),
        out_specs=[IN_VMEM] * 2,
        out_shape=[jax.ShapeDtypeStruct((columns // 2, size), BF16)] * 2,
        scratch_shapes=[
            pltpu.VMEM((columns, rows), BF16),
            pltpu.VMEM((rows, size), BF16),
            pltpu.SemaphoreType.DMA((len(parts) + 1,)),
        ],
        compiler_params=pltpu.CompilerParams(vmem_limit_bytes=VMEM),
        cost_estimate=pl.CostEstimate(flops=2 * size * columns * rows, bytes_accessed=2 * rows * size, transcendentals=0),
    )(current, *arrays)


class Panel:
    def __init__(self, p, current, m):
        self.p, self.current, self.m = p, current, m
        self.groups, self.coeffs = [], []

    def take(self, parts, early=(), late=()):
        mine, other = coeff(after(self.current, *early), parts)
        self.coeffs += sum_rows(mine, other, self.m, late)
        self.groups.append(parts)
        return self.coeffs[-2:]

    def update(self, factors, last):
        columns, rows = self.current.shape
        size = factors.shape[1]
        parts = [part for group in self.groups for part in group]
        arrays = [x for part in parts for x in part.arrays]
        n_copies = 1 + 2 * sum(len(part.blocks) for part in parts) + size // 256
        flops = 2 * size * columns * (size + rows)
        return pl.pallas_call(
            functools.partial(update_kernel, self.p, last, self.groups, parts),
            in_specs=[ANY] * (2 + len(self.coeffs) + len(arrays)),
            out_specs=IN_VMEM,
            out_shape=jax.ShapeDtypeStruct((rows, columns) if last else (columns, rows), BF16),
            scratch_shapes=[
                pltpu.VMEM((size, size), BF16),
                pltpu.VMEM((columns, size), BF16),
                pltpu.VMEM((columns, size), BF16),
                pltpu.VMEM((columns, size), BF16),
                pltpu.VMEM((columns, rows), BF16),
                pltpu.VMEM((rows, size), BF16),
                pltpu.SemaphoreType.DMA((n_copies,)),
                pltpu.SemaphoreType.DMA((len(parts),)),
            ],
            compiler_params=pltpu.CompilerParams(vmem_limit_bytes=VMEM),
            cost_estimate=pl.CostEstimate(flops=flops, bytes_accessed=2 * size * (size + rows), transcendentals=0),
        )(factors, self.current, *self.coeffs, *arrays)


class Line:
    def __init__(self, own, n):
        self.own, self.n, self.even, self.odd = own, n, {}, {}

    def pairs(self, s, parity):
        out = []
        for i in range(parity, self.n - 1, 2):
            out += [(i, i + 1)] if i - s + 1 >= 0 else []
            out += [(i + 1, i)] if i + s < self.n else []
        return out

    def send(self, x, pairs, ready):
        return lax.ppermute(after(x, *ready), "vecs", pairs) if x is not None and pairs else None

    def send_even(self, s, ready):
        self.even[s] = self.send(self.own if s == 1 else self.odd[s - 1], self.pairs(s, 0), ready)
        return held(self.even[s])

    def send_odd(self, s, ready):
        self.odd[s] = self.send(self.own if s == 1 else self.even[s - 1], self.pairs(s, 1), ready)
        return held(self.odd[s])

    def part(self, g):
        n, wide = self.n, self.own.shape[1]

        def index(z, s, parity):
            return jnp.where(z % 2 == parity, z + s, z - s)

        if g == 0:
            return Part([self.own], [(lambda z: z * wide, 0, wide)])
        if g == 1:
            return Part([self.even[1]], [(lambda z: index(z, 1, 0) * wide, 0, wide)])
        s = g - 1
        c = n - s - 1 if s % 2 else n - s + 1

        def here(z):
            i = index(z, s, 1)
            return (i >= 0) & (i < n)

        place = lambda z: jnp.where(here(z), index(z, s, 1), index(z, c, 0)) * wide
        return Part([self.odd[s], self.even[c]], [(place, 0, wide)], here)


def body(n, m, eigvecs, reflectors, factors):
    p1 = reflectors[1]
    p0 = after(reflectors, p1)[0]
    one, zero = Line(p1, n), Line(p0, n)
    panel1 = Panel(1, after(eigvecs, p1).T, m)
    end1 = 3
    ready = []
    for w in range(1, 2 * n - 2):
        got = []
        if w < n:
            got += one.send_even(w, ready) + one.send_odd(w, ready)
        if w == 2:
            zero.send_even(1, ready)
        if w == n - 1:
            got += zero.send_odd(1, ready)
        if 2 <= w - n + 2 < n:
            got += zero.send_even(w - n + 2, ready) + zero.send_odd(w - n + 2, ready)
        if w == n - 1:
            got += panel1.take([one.part(g) for g in range(n) if g != end1], ready, got)
        if w == n:
            got += panel1.take([one.part(end1)], ready)
        if w == n + 1:
            panel0 = Panel(0, after(panel1.update(factors, False), *ready), m)
        if w == 2 * n - 3:
            panel0.take([zero.part(g) for g in range(n) if g != end1], ready, got)
        ready = got
    panel0.take([zero.part(end1)], ready)
    return panel0.update(factors, True)


def plain_body(n, m, eigvecs, reflectors, factors):
    current = eigvecs
    for p in (1, 0):
        panel = lax.all_gather(reflectors[p], "vecs", axis=1, tiled=True)
        mine, other = jnp.split(dot(current, panel, 0, 0).astype(BF16), 2)
        odd = lax.axis_index("rows") % 2 == 1
        mine, other = sum_rows(jnp.where(odd, other, mine), jnp.where(odd, mine, other), m)
        total = jnp.where(odd, jnp.concatenate([other, mine]), jnp.concatenate([mine, other]))
        scaled = dot(factors[p], total, 1, 1).astype(BF16)
        current = (current.astype(F32) - dot(panel, scaled, 1, 0)).astype(BF16)
    return current


def solution(mesh):
    n, m = mesh.shape["vecs"], mesh.shape["rows"]

    def local(eigvecs, reflectors, factors):
        wide, columns, size = reflectors.shape[2], eigvecs.shape[1], factors.shape[1]
        fits = wide % 256 == 0 and columns % 32 == 0 and size % 256 == 0 and n % 2 == 0 and n >= 4
        return (body if fits else plain_body)(n, m, eigvecs, reflectors, factors)

    in_specs = (P("rows", "vecs"), P(None, "rows", "vecs"), P())
    out_specs = P("rows", "vecs")
    return jax.shard_map(local, mesh=mesh, in_specs=in_specs, out_specs=out_specs, check_vma=False)
```

```python
import functools

import jax
import jax.numpy as jnp
from jax import lax
from jax.experimental import pallas as pl
from jax.experimental.pallas import tpu as pltpu
from jax.sharding import PartitionSpec as P

F32, BF16 = jnp.float32, jnp.bfloat16
VMEM = 16 << 20
ANY = pl.BlockSpec(memory_space=pl.ANY)
IN_VMEM = pl.BlockSpec(memory_space=pltpu.VMEM)


def after(x, *others):
    return lax.optimization_barrier((x,) + others)[0]


def held(*xs):
    return [x for x in xs if x is not None]


def dot(a, b, ca, cb):
    return lax.dot_general(a, b, (((ca,), (cb,)), ((), ())), preferred_element_type=F32)


def swap(x, bit, m):
    return lax.ppermute(x, "rows", [(i, i ^ bit) for i in range(m)])


class Part:
    def __init__(self, arrays, blocks, here=None):
        self.arrays, self.blocks, self.here = arrays, blocks, here
        self.rows, self.width = [x.shape[0] for x in arrays], arrays[0].shape[1]


def start_parts(parts, refs, panels, sems):
    waits, at, column = [], 0, 0
    for k, part in enumerate(parts):
        columns = pl.ds(column, part.width)
        whole = pltpu.make_async_copy(refs[at], panels.at[:, columns], sems.at[k])
        if part.here is None:
            whole.start()
        else:
            here = part.here(lax.axis_index("vecs"))
            pl.when(here)(whole.start)
            row = 0
            for i, rows in enumerate(part.rows[1:]):
                place = panels.at[pl.ds(row, rows), columns]
                piece = pltpu.make_async_copy(refs[at + 1 + i], place, sems.at[k])
                pl.when(jnp.logical_not(here))(piece.start)
                row += rows
        waits.append(whole.wait)
        at += len(part.rows)
        column += part.width
    return waits


def coeff_kernel(parts, current_ref, *refs):
    n = sum(len(part.rows) for part in parts)
    mine_ref, other_ref, current, panels, sems = refs[n:]
    copy = pltpu.make_async_copy(current_ref, current, sems.at[len(parts)])
    copy.start()
    waits = start_parts(parts, refs[:n], panels, sems)
    copy.wait()
    half = current.shape[0] // 2
    odd = lax.axis_index("rows") % 2 == 1
    column = 0
    for part, wait in zip(parts, waits):
        wait()
        at = slice(column, column + part.width)
        total = dot(current[...], panels[:, at], 1, 0)
        mine_ref[:, at] = jnp.where(odd, total[half:], total[:half]).astype(BF16)
        other_ref[:, at] = jnp.where(odd, total[:half], total[half:]).astype(BF16)
        column += part.width


class Copies:
    def __init__(self, sems):
        self.sems, self.count = sems, 0

    def __call__(self, source, target):
        copy = pltpu.make_async_copy(source, target, self.sems.at[self.count])
        self.count += 1
        copy.start()
        return copy.wait


def columns_at(place, width):
    return pl.ds(pl.multiple_of(place(lax.axis_index("vecs")), width), width)


def half_rows(whose, half):
    own = lax.axis_index("rows") % 2
    return pl.ds(pl.multiple_of(jnp.where(own == whose, 0, half), half), half)


def scale_kernel(p, groups, factors_ref, *refs):
    coeff_refs, (out_ref, factor, coeff, sems) = refs[: 2 * len(groups)], refs[2 * len(groups) :]
    size, half = factor.shape[0], coeff.shape[0] // 2
    copy = Copies(sems)
    tiles = []
    for t in reversed(range(0, size, 256)):
        rows, cols = pl.ds(t, 256), pl.ds(t, size - t)
        tiles.append((t, copy(factors_ref.at[p, rows, cols], factor.at[rows, cols])))
    coeff[...] = jnp.zeros_like(coeff)
    waits = []
    for k, ref in enumerate(coeff_refs):
        at = 0
        for part in groups[k // 2]:
            for place, offset, width in part.blocks:
                target = coeff.at[half_rows(k % 2, half), columns_at(place, width)]
                waits.append(copy(ref.at[:, pl.ds(at + offset, width)], target))
            at += part.width
    for wait in waits:
        wait()
    plain = coeff[...].T
    for t, wait in tiles:
        wait()
        out_ref[t : t + 256] = dot(factor[t : t + 256, t:], plain[t:], 1, 0).astype(BF16)


def prepare_kernel(p, last, parts, late, factors_ref, current_ref, scaled_ref, *refs):
    n = sum(len(part.rows) for part in parts)
    rest_ref, across_ref, current, met, panels, sems, panel_sems = refs[n:]
    columns = current.shape[0]
    copy = Copies(sems)
    parts_there = start_parts(parts, refs[:n], panels, panel_sems)
    waits = [copy(current_ref, current)]
    at = 0
    for part in parts:
        for place, offset, width in part.blocks:
            rows, there = pl.ds(at + offset, width), columns_at(place, width)
            waits.append(copy(scaled_ref.at[there], met.at[rows, pl.ds(0, columns)]))
            to = columns
            for other in late:
                for other_place, other_offset, other_width in other.blocks:
                    source = factors_ref.at[p, there, columns_at(other_place, other_width)]
                    waits.append(copy(source, met.at[rows, pl.ds(to + other_offset, other_width)]))
                to += other.width
        at += part.width
    for wait in waits + parts_there:
        wait()
    product = dot(panels[...], met[...], 1, 0)
    across_ref[...] = product[:, columns:].astype(BF16)
    if last:
        rest_ref[...] = current[...].astype(F32).T - product[:, :columns]
    else:
        rest_ref[...] = current[...].astype(F32) - product[:, :columns].T


def finish_kernel(last, rest_ref, across_ref, own_ref, other_ref, out_ref, rest, across, coeff, sems):
    copy = Copies(sems)
    half = coeff.shape[0] // 2
    waits = [copy(rest_ref, rest), copy(across_ref, across)]
    waits += [copy(ref, coeff.at[half_rows(k, half)]) for k, ref in enumerate((own_ref, other_ref))]
    for wait in waits:
        wait()
    product = dot(across[...], coeff[...], 1, 1) if last else dot(coeff[...], across[...], 1, 1)
    out_ref[...] = (rest[...] - product).astype(BF16)


def call(kernel, inputs, outs, scratch, flops):
    return pl.pallas_call(
        kernel,
        in_specs=[ANY] * len(inputs),
        out_specs=[IN_VMEM] * len(outs),
        out_shape=[jax.ShapeDtypeStruct(shape, dtype) for shape, dtype in outs],
        scratch_shapes=scratch,
        compiler_params=pltpu.CompilerParams(vmem_limit_bytes=VMEM),
        cost_estimate=pl.CostEstimate(
            flops=flops, bytes_accessed=sum(x.size * x.dtype.itemsize for x in inputs), transcendentals=0
        ),
    )(*inputs)


def arrays_of(parts):
    return [x for part in parts for x in part.arrays]


def scale(p, factors, groups, coeffs):
    size, columns = factors.shape[1], 2 * coeffs[0].shape[0]
    n_copies = size // 256 + 2 * sum(len(part.blocks) for group in groups for part in group)
    scratch = [
        pltpu.VMEM((size, size), BF16),
        pltpu.VMEM((columns, size), BF16),
        pltpu.SemaphoreType.DMA((n_copies,)),
    ]
    kernel = functools.partial(scale_kernel, p, groups)
    return call(kernel, [factors, *coeffs], [((size, columns), BF16)], scratch, size * size * columns)[0]


def prepare(p, last, factors, current, scaled, parts, late):
    columns, rows = current.shape
    size = factors.shape[1]
    more = sum(part.width for part in late)
    n_copies = 1 + sum(len(part.blocks) for part in parts) * (1 + sum(len(part.blocks) for part in late))
    scratch = [
        pltpu.VMEM((columns, rows), BF16),
        pltpu.VMEM((size, columns + more), BF16),
        pltpu.VMEM((rows, size), BF16),
        pltpu.SemaphoreType.DMA((n_copies,)),
        pltpu.SemaphoreType.DMA((len(parts),)),
    ]
    outs = [((rows, columns) if last else (columns, rows), F32), ((rows, more), BF16)]
    kernel = functools.partial(prepare_kernel, p, last, parts, late)
    inputs = [factors, current, scaled, *arrays_of(parts)]
    return call(kernel, inputs, outs, scratch, 2 * rows * size * (columns + more))


def finish(last, rest, across, coeffs):
    rows, more = across.shape
    columns = rest.size // rows
    scratch = [
        pltpu.VMEM(rest.shape, F32),
        pltpu.VMEM(across.shape, BF16),
        pltpu.VMEM((columns, more), BF16),
        pltpu.SemaphoreType.DMA((4,)),
    ]
    kernel = functools.partial(finish_kernel, last)
    return call(kernel, [rest, across, *coeffs], [(rest.shape, BF16)], scratch, 2 * rows * more * columns)[0]


def coeff(current, parts):
    columns, rows = current.shape
    size = sum(part.width for part in parts)
    arrays = [x for part in parts for x in part.arrays]
    return pl.pallas_call(
        functools.partial(coeff_kernel, parts),
        in_specs=[ANY] * (1 + len(arrays)),
        out_specs=[IN_VMEM] * 2,
        out_shape=[jax.ShapeDtypeStruct((columns // 2, size), BF16)] * 2,
        scratch_shapes=[
            pltpu.VMEM((columns, rows), BF16),
            pltpu.VMEM((rows, size), BF16),
            pltpu.SemaphoreType.DMA((len(parts) + 1,)),
        ],
        compiler_params=pltpu.CompilerParams(vmem_limit_bytes=VMEM),
        cost_estimate=pl.CostEstimate(flops=2 * size * columns * rows, bytes_accessed=2 * rows * size, transcendentals=0),
    )(current, *arrays)


GROUPS = {1: ((0, 1, 2), (3,)), 0: ((0, 1, 2), (3,))}
PIECES = {"O": 1, "F3": 1}
JOINED = "swap"
GATES = {
    "P0": ("p1",),
    "X": ("p1",),
    "E2": ("M1",),
    "M2": ("M1",),
    "E3": ("E2",),
    "N1": ("E2", "M2"),
    "c1.0": ("E3", "N1"),
    "a1.0": ("E2", "M2"),
    "a1.1": ("d1.0", "N1"),
    "N2": ("d1.0", "E3"),
    "F2": ("d1.0", "E3"),
    "F3": ("F2",),
    "a0.0": ("N2", "F2"),
    "c0.0": ("F3",),
}


class Steps:
    def __init__(self, n, m, eigvecs, reflectors, factors):
        self.n, self.m, self.factors = n, m, factors
        self.eigvecs, self.reflectors = eigvecs, reflectors
        self.z = lax.axis_index("vecs")
        self.made = {}

    def __call__(self, name):
        if name not in self.made:
            self.made[name] = None
            self.made[name] = self.make(name)
        if self.made[name] is None:
            raise ValueError("circular gates")
        return self.made[name]

    def gated(self, name, x):
        others = []
        for other in GATES.get(name, ()):
            got = self(other)
            others += list(got) if isinstance(got, (tuple, list)) else [got]
        return after(x, *others) if others else x

    def send(self, name, x, pairs):
        return lax.ppermute(self.gated(name, x), "vecs", pairs)

    def pieces(self, name, x, pairs):
        size = x.shape[0] // PIECES[name]
        return [self.send(name, x[k * size : (k + 1) * size], pairs) for k in range(PIECES[name])]

    def make(self, name):
        n, z = self.n, self.z
        outer = [(i, i ^ 1) for i in range(n)]
        inward, outward = [(0, 1), (n - 1, n - 2)], [(1, 0), (n - 2, n - 1)]
        middle, skip = [(1, 2), (2, 1)], [(2, 0), (n - 3, n - 1)]
        at_end = (z == 0) | (z == n - 1)
        if name == "p1":
            return self.reflectors[1]
        if name == "P0":
            return self.gated(name, self.reflectors)[0]
        if name == "X":
            return self.gated(name, self.eigvecs).T
        if name == "E1":
            return self.send(name, self("p1"), outer)
        if name == "M1":
            return self.send(name, self("p1"), middle)
        if name == "E2":
            if JOINED == "E2":
                return self.send(name, jnp.where(at_end, self("P0"), self("M1")), outer)
            return self.send(name, self("M1"), outward)
        if name == "M2":
            return self.send(name, self("E1"), middle)
        if name == "E3":
            return self.send(name, self("M2"), outward)
        if name == "E3s":
            return self.send(name, self("E1"), skip)
        if name == "I":
            if JOINED == "E2":
                return self("E2")
            return self.send(name, self("P0"), outer if JOINED == "swap" else inward)
        if name == "O":
            return self.pieces(name, self("P0"), outward)
        if name == "N1":
            return self.send(name, self("P0"), middle)
        if name == "N2":
            return self.send(name, self("I"), middle)
        if name == "F2":
            return self.send(name, self("N1"), outward)
        if name == "F3":
            return self.pieces(name, self("N2"), outward)
        step, p = name[0], int(name[1])
        groups = [[self.part(p, g) for g in group] for group in GROUPS[p]]
        late = len(groups) - 1
        if step == "S":
            coeffs = [self(f"{what}{p}.{k}") for k in range(late) for what in "cd"]
            return scale(p, self.gated(name, self.factors), groups[:late], coeffs)
        if step == "Y":
            current = self.gated(name, self("X" if p else "U1"))
            return prepare(p, p == 0, self.factors, current, self(f"S{p}"), sum(groups, []), groups[late])
        if step == "U":
            rest, across = self(f"Y{p}")
            coeffs = [self(f"{what}{p}.{late}") for what in "cd"]
            return finish(p == 0, self.gated(name, rest), across, coeffs)
        k = int(name[3:])
        if step == "a":
            return coeff(self.gated(name, self("U1" if p == 0 else "X")), groups[k])
        if step == "b":
            mine, other = self("a" + name[1:])
            got = self.gated(name, swap(other, 1, self.m))
            return (mine.astype(F32) + got.astype(F32)).astype(BF16)
        if step == "c":
            mine, bit = self("b" + name[1:]), 2
            while bit < self.m:
                got = [swap(mine, s * bit, self.m) for s in range(1, 4) if s * bit < self.m]
                mine = sum([self.gated(name, g).astype(F32) for g in got], mine.astype(F32)).astype(BF16)
                bit *= 4
            return mine
        return swap(self.gated(name, self("c" + name[1:])), 1, self.m)

    def part(self, p, g):
        n, wide = self.n, self.reflectors.shape[2]

        def inner(z):
            return (z > 0) & (z < n - 1)

        places = (
            lambda z: z,
            lambda z: z + 1 - 2 * (z % 2),
            lambda z: jnp.where(inner(z), n - 1 - z, (z + 2) % n),
            lambda z: jnp.where(inner(z), (z + 2) % n, n - 1 - z),
        )
        if p == 1:
            arrays = (["p1"], ["E1"], ["M1", "E2"], ["M2", "E3"])[g]
        else:
            arrays = (["P0"], ["I"] if JOINED == "swap" else ["I", "O"], ["N1", "F2"], ["N2", "F3"])[g]
        found = []
        for name in arrays:
            got = self(name)
            found += got if isinstance(got, list) else [got]
        blocks = [(lambda z: places[g](z) * wide, 0, wide)]
        return Part(found, blocks, inner if len(found) > 1 else None)


def swap_sum(mine, other, m):
    mine = (mine.astype(F32) + swap(other, 1, m).astype(F32)).astype(BF16)
    bit = 2
    while bit < m:
        got = [swap(mine, s * bit, m) for s in range(1, 4) if s * bit < m]
        mine = sum([g.astype(F32) for g in got], mine.astype(F32)).astype(BF16)
        bit *= 4
    return mine, swap(mine, 1, m)


def plain_body(n, m, eigvecs, reflectors, factors):
    current = eigvecs
    for p in (1, 0):
        panel = lax.all_gather(reflectors[p], "vecs", axis=1, tiled=True)
        mine, other = jnp.split(dot(current, panel, 0, 0).astype(BF16), 2)
        odd = lax.axis_index("rows") % 2 == 1
        mine, other = swap_sum(jnp.where(odd, other, mine), jnp.where(odd, mine, other), m)
        total = jnp.where(odd, jnp.concatenate([other, mine]), jnp.concatenate([mine, other]))
        scaled = dot(factors[p], total, 1, 1).astype(BF16)
        current = (current.astype(F32) - dot(panel, scaled, 1, 0)).astype(BF16)
    return current


def solution(mesh):
    n, m = mesh.shape["vecs"], mesh.shape["rows"]

    def local(eigvecs, reflectors, factors):
        wide, columns, size = reflectors.shape[2], eigvecs.shape[1], factors.shape[1]
        fits = n == 4 and wide % 128 == 0 and columns % 32 == 0 and size % 256 == 0
        if fits:
            return Steps(n, m, eigvecs, reflectors, factors)("U0")
        return plain_body(n, m, eigvecs, reflectors, factors)

    in_specs = (P("rows", "vecs"), P(None, "rows", "vecs"), P())
    out_specs = P("rows", "vecs")
    return jax.shard_map(local, mesh=mesh, in_specs=in_specs, out_specs=out_specs, check_vma=False)
```

```python
import functools

import jax
import jax.numpy as jnp
from jax import lax
from jax.experimental import pallas as pl
from jax.experimental.pallas import tpu as pltpu
from jax.sharding import PartitionSpec as P

F32, BF16 = jnp.float32, jnp.bfloat16
VMEM = 16 << 20
ANY = pl.BlockSpec(memory_space=pl.ANY)
IN_VMEM = pl.BlockSpec(memory_space=pltpu.VMEM)


def after(x, *others):
    return lax.optimization_barrier((x,) + others)[0]


def held(*xs):
    return [x for x in xs if x is not None]


def dot(a, b, ca, cb):
    return lax.dot_general(a, b, (((ca,), (cb,)), ((), ())), preferred_element_type=F32)


def swap(x, bit, m):
    return lax.ppermute(x, "rows", [(i, i ^ bit) for i in range(m)])


class Part:
    def __init__(self, p, arrays, blocks, here=None):
        self.arrays, self.blocks, self.here = arrays, blocks, here
        self.leads = [p if x.ndim == 3 else None for x in arrays]
        self.rows, self.width = [x.shape[-2] for x in arrays], arrays[0].shape[-1]


def start_parts(parts, refs, panels, sems):
    waits, at, column = [], 0, 0
    for k, part in enumerate(parts):
        columns = pl.ds(column, part.width)
        own = [ref if p is None else ref.at[p] for ref, p in zip(refs[at : at + len(part.rows)], part.leads)]
        whole = pltpu.make_async_copy(own[0], panels.at[:, columns], sems.at[k])
        if part.here is None:
            whole.start()
        else:
            here = part.here(lax.axis_index("vecs"))
            pl.when(here)(whole.start)
            row = 0
            for i, rows in enumerate(part.rows[1:]):
                place = panels.at[pl.ds(row, rows), columns]
                piece = pltpu.make_async_copy(own[1 + i], place, sems.at[k])
                pl.when(jnp.logical_not(here))(piece.start)
                row += rows
        waits.append(whole.wait)
        at += len(part.rows)
        column += part.width
    return waits


def coeff_kernel(parts, current_ref, *refs):
    n = sum(len(part.rows) for part in parts)
    mine_ref, other_ref, current, panels, sems = refs[n:]
    copy = pltpu.make_async_copy(current_ref, current, sems.at[len(parts)])
    copy.start()
    waits = start_parts(parts, refs[:n], panels, sems)
    copy.wait()
    half = current.shape[0] // 2
    odd = lax.axis_index("rows") % 2 == 1
    column = 0
    for part, wait in zip(parts, waits):
        wait()
        at = slice(column, column + part.width)
        total = dot(current[...], panels[:, at], 1, 0)
        mine_ref[:, at] = jnp.where(odd, total[half:], total[:half]).astype(BF16)
        other_ref[:, at] = jnp.where(odd, total[:half], total[half:]).astype(BF16)
        column += part.width


class Copies:
    def __init__(self, sems):
        self.sems, self.count = sems, 0

    def __call__(self, source, target):
        copy = pltpu.make_async_copy(source, target, self.sems.at[self.count])
        self.count += 1
        copy.start()
        return copy.wait


def columns_at(place, width):
    return pl.ds(pl.multiple_of(place(lax.axis_index("vecs")), width), width)


def half_rows(whose, half):
    own = lax.axis_index("rows") % 2
    return pl.ds(pl.multiple_of(jnp.where(own == whose, 0, half), half), half)


def scale_kernel(p, groups, factors_ref, *refs):
    coeff_refs, (out_ref, factor, coeff, sems) = refs[: 2 * len(groups)], refs[2 * len(groups) :]
    size, half = factor.shape[0], coeff.shape[0] // 2
    copy = Copies(sems)
    tiles = []
    for t in reversed(range(0, size, 256)):
        rows, cols = pl.ds(t, 256), pl.ds(t, size - t)
        tiles.append((t, copy(factors_ref.at[p, rows, cols], factor.at[rows, cols])))
    coeff[...] = jnp.zeros_like(coeff)
    waits = []
    for k, ref in enumerate(coeff_refs):
        at = 0
        for part in groups[k // 2]:
            for place, offset, width in part.blocks:
                target = coeff.at[half_rows(k % 2, half), columns_at(place, width)]
                waits.append(copy(ref.at[:, pl.ds(at + offset, width)], target))
            at += part.width
    for wait in waits:
        wait()
    plain = coeff[...].T
    for t, wait in tiles:
        wait()
        out_ref[t : t + 256] = dot(factor[t : t + 256, t:], plain[t:], 1, 0).astype(BF16)


def prepare_kernel(p, last, parts, late, factors_ref, current_ref, scaled_ref, *refs):
    n = sum(len(part.rows) for part in parts)
    rest_ref, across_ref, current, met, panels, sems, panel_sems = refs[n:]
    columns = current.shape[0]
    copy = Copies(sems)
    parts_there = start_parts(parts, refs[:n], panels, panel_sems)
    waits = [copy(current_ref, current)]
    at = 0
    for part in parts:
        for place, offset, width in part.blocks:
            rows, there = pl.ds(at + offset, width), columns_at(place, width)
            waits.append(copy(scaled_ref.at[there], met.at[rows, pl.ds(0, columns)]))
            to = columns
            for other in late:
                for other_place, other_offset, other_width in other.blocks:
                    source = factors_ref.at[p, there, columns_at(other_place, other_width)]
                    waits.append(copy(source, met.at[rows, pl.ds(to + other_offset, other_width)]))
                to += other.width
        at += part.width
    for wait in waits + parts_there:
        wait()
    product = dot(panels[...], met[...], 1, 0)
    across_ref[...] = product[:, columns:].astype(BF16)
    if last:
        rest_ref[...] = current[...].astype(F32).T - product[:, :columns]
    else:
        rest_ref[...] = current[...].astype(F32) - product[:, :columns].T


def finish_kernel(last, rest_ref, across_ref, own_ref, other_ref, out_ref, rest, across, coeff, sems):
    copy = Copies(sems)
    half = coeff.shape[0] // 2
    waits = [copy(rest_ref, rest), copy(across_ref, across)]
    waits += [copy(ref, coeff.at[half_rows(k, half)]) for k, ref in enumerate((own_ref, other_ref))]
    for wait in waits:
        wait()
    product = dot(across[...], coeff[...], 1, 1) if last else dot(coeff[...], across[...], 1, 1)
    out_ref[...] = (rest[...] - product).astype(BF16)


def call(kernel, inputs, outs, scratch, flops):
    return pl.pallas_call(
        kernel,
        in_specs=[ANY] * len(inputs),
        out_specs=[IN_VMEM] * len(outs),
        out_shape=[jax.ShapeDtypeStruct(shape, dtype) for shape, dtype in outs],
        scratch_shapes=scratch,
        compiler_params=pltpu.CompilerParams(vmem_limit_bytes=VMEM),
        cost_estimate=pl.CostEstimate(
            flops=flops, bytes_accessed=sum(x.size * x.dtype.itemsize for x in inputs), transcendentals=0
        ),
    )(*inputs)


def arrays_of(parts):
    return [x for part in parts for x in part.arrays]


def scale(p, factors, groups, coeffs):
    size, columns = factors.shape[1], 2 * coeffs[0].shape[0]
    n_copies = size // 256 + 2 * sum(len(part.blocks) for group in groups for part in group)
    scratch = [
        pltpu.VMEM((size, size), BF16),
        pltpu.VMEM((columns, size), BF16),
        pltpu.SemaphoreType.DMA((n_copies,)),
    ]
    kernel = functools.partial(scale_kernel, p, groups)
    return call(kernel, [factors, *coeffs], [((size, columns), BF16)], scratch, size * size * columns)[0]


def prepare(p, last, factors, current, scaled, parts, late):
    columns, rows = current.shape
    size = factors.shape[1]
    more = sum(part.width for part in late)
    n_copies = 1 + sum(len(part.blocks) for part in parts) * (1 + sum(len(part.blocks) for part in late))
    scratch = [
        pltpu.VMEM((columns, rows), BF16),
        pltpu.VMEM((size, columns + more), BF16),
        pltpu.VMEM((rows, size), BF16),
        pltpu.SemaphoreType.DMA((n_copies,)),
        pltpu.SemaphoreType.DMA((len(parts),)),
    ]
    outs = [((rows, columns) if last else (columns, rows), F32), ((rows, more), BF16)]
    kernel = functools.partial(prepare_kernel, p, last, parts, late)
    inputs = [factors, current, scaled, *arrays_of(parts)]
    return call(kernel, inputs, outs, scratch, 2 * rows * size * (columns + more))


def finish(last, rest, across, coeffs):
    rows, more = across.shape
    columns = rest.size // rows
    scratch = [
        pltpu.VMEM(rest.shape, F32),
        pltpu.VMEM(across.shape, BF16),
        pltpu.VMEM((columns, more), BF16),
        pltpu.SemaphoreType.DMA((4,)),
    ]
    kernel = functools.partial(finish_kernel, last)
    return call(kernel, [rest, across, *coeffs], [(rest.shape, BF16)], scratch, 2 * rows * more * columns)[0]


def coeff(current, parts):
    columns, rows = current.shape
    size = sum(part.width for part in parts)
    arrays = [x for part in parts for x in part.arrays]
    return pl.pallas_call(
        functools.partial(coeff_kernel, parts),
        in_specs=[ANY] * (1 + len(arrays)),
        out_specs=[IN_VMEM] * 2,
        out_shape=[jax.ShapeDtypeStruct((columns // 2, size), BF16)] * 2,
        scratch_shapes=[
            pltpu.VMEM((columns, rows), BF16),
            pltpu.VMEM((rows, size), BF16),
            pltpu.SemaphoreType.DMA((len(parts) + 1,)),
        ],
        compiler_params=pltpu.CompilerParams(vmem_limit_bytes=VMEM),
        cost_estimate=pl.CostEstimate(flops=2 * size * columns * rows, bytes_accessed=2 * rows * size, transcendentals=0),
    )(current, *arrays)


GROUPS = {1: ((0, 1), (2, 3)), 0: ((0, 1, 2), (3,))}
PIECES = {'O': 1, 'F3': 1}
JOINED = 'swap'
WHOLE = ()
DIRECT = ('0.0', '0.1', '0.2', '1.0', '1.1', '1.2')
SKIP = ('E3',)
GATES = {
    'X': ('p1',),
    'd1.0': ('I',),
    'a1.1': ('E3',),
    'c1.1': ('N2', 'F2', 'Y1'),
    'c0.1': ('Y0', 'F2'),
    'U1': ('N2',),
    'd0.1': ('N1',),
}


class Steps:
    def __init__(self, n, m, eigvecs, reflectors, factors):
        self.n, self.m, self.factors = n, m, factors
        self.eigvecs, self.reflectors = eigvecs, reflectors
        self.z = lax.axis_index("vecs")
        self.made = {}

    def __call__(self, name):
        if name not in self.made:
            self.made[name] = None
            self.made[name] = self.make(name)
        if self.made[name] is None:
            raise ValueError("circular gates")
        return self.made[name]

    def gated(self, name, x):
        others = []
        for other in GATES.get(name, ()):
            got = self(other)
            others += list(got) if isinstance(got, (tuple, list)) else [got]
        return after(x, *others) if others else x

    def send(self, name, x, pairs):
        return lax.ppermute(self.gated(name, x), "vecs", pairs)

    def pieces(self, name, x, pairs):
        size = x.shape[0] // PIECES[name]
        return [self.send(name, x[k * size : (k + 1) * size], pairs) for k in range(PIECES[name])]

    def make(self, name):
        n, z = self.n, self.z
        outer = [(i, i ^ 1) for i in range(n)]
        inward, outward = [(0, 1), (n - 1, n - 2)], [(1, 0), (n - 2, n - 1)]
        middle, skip = [(1, 2), (2, 1)], [(2, 0), (n - 3, n - 1)]
        at_end = (z == 0) | (z == n - 1)
        if name == "p1":
            return self.reflectors[1]
        if name == "P0":
            return self.gated(name, self.reflectors)[0]
        if name == "X":
            return self.gated(name, self.eigvecs).T
        if name in WHOLE:
            source = self.reflectors if name[1] == "1" else self({"E2": "M1", "M2": "E1"}[name])
            return self.send(name, source, middle if name[0] == "M" else outer if name == "E1" else outward)
        if name in ("E1", "M1", "E2", "M2", "E3"):
            if name in SKIP:
                return self.send(name, self.panel(1, "E1"), skip)
            source = {"E1": "p1", "M1": "p1", "E2": "M1", "M2": "E1", "E3": "M2"}[name]
            if name == "E2" and JOINED == "E2":
                return self.send(name, jnp.where(at_end, self("P0"), self.panel(1, "M1")), outer)
            return self.send(name, self.panel(1, source), {"E1": outer, "M1": middle, "M2": middle}.get(name, outward))
        twin = {"I": "E1", "N1": "M1", "F2": "E2", "N2": "M2"}.get(name)
        if twin in WHOLE:
            return self(twin)
        if name == "I":
            if JOINED == "E2":
                return self("E2")
            return self.send(name, self("P0"), outer if JOINED == "swap" else inward)
        if name == "O":
            return self.pieces(name, self("P0"), outward)
        if name in ("N1", "N2", "F2"):
            source = {"N1": "P0", "N2": "I", "F2": "N1"}[name]
            return self.send(name, self.panel(0, source), outward if name == "F2" else middle)
        if name == "F3":
            if name in SKIP:
                return self.pieces(name, self.panel(0, "I"), skip)
            return self.pieces(name, self.panel(0, "N2"), outward)
        step, p = name[0], int(name[1])
        groups = [[self.part(p, g) for g in group] for group in GROUPS[p]]
        late = len(groups) - 1
        if step == "S":
            coeffs = [self(f"{what}{p}.{k}") for k in range(late) for what in "cd"]
            return scale(p, self.gated(name, self.factors), groups[:late], coeffs)
        if step == "Y":
            current = self.gated(name, self("X" if p else "U1"))
            return prepare(p, p == 0, self.factors, current, self(f"S{p}"), sum(groups, []), groups[late])
        if step == "U":
            rest, across = self(f"Y{p}")
            coeffs = [self(f"{what}{p}.{late}") for what in "cd"]
            return finish(p == 0, self.gated(name, rest), across, coeffs)
        k = int(name[3:])
        if step == "a":
            return coeff(self.gated(name, self("U1" if p == 0 else "X")), groups[k])
        if step == "b":
            mine, other = self("a" + name[1:])
            got = self.gated(name, swap(other, 1, self.m))
            return (mine.astype(F32) + got.astype(F32)).astype(BF16)
        if step == "c":
            mine, bit = self("b" + name[1:]), 2
            while bit < self.m:
                if name[1:] in DIRECT or 2 * bit >= self.m:
                    got = [swap(mine, s * bit, self.m) for s in range(1, 4) if s * bit < self.m]
                    mine = sum([self.gated(name, g).astype(F32) for g in got], mine.astype(F32)).astype(BF16)
                else:
                    halves = jnp.split(mine, 2)
                    for bits in ((bit, 2 * bit), (2 * bit, bit)):
                        got = [swap(x, b, self.m) for x, b in zip(halves, bits)]
                        if bits[0] > bit:
                            got = [self.gated(name, g) for g in got]
                        halves = [(x.astype(F32) + g.astype(F32)).astype(BF16) for x, g in zip(halves, got)]
                    mine = jnp.concatenate(halves)
                bit *= 4
            return mine
        return swap(self.gated(name, self("c" + name[1:])), 1, self.m)

    def panel(self, p, name):
        x = self(name)
        return x[p] if x.ndim == 3 else x

    def part(self, p, g):
        n, wide = self.n, self.reflectors.shape[2]

        def inner(z):
            return (z > 0) & (z < n - 1)

        places = (
            lambda z: z,
            lambda z: z + 1 - 2 * (z % 2),
            lambda z: jnp.where(inner(z), n - 1 - z, (z + 2) % n),
            lambda z: jnp.where(inner(z), (z + 2) % n, n - 1 - z),
        )
        if p == 1:
            arrays = (["p1"], ["E1"], ["M1", "E2"], ["M2", "E3"])[g]
        else:
            together = JOINED == "swap" or "E1" in WHOLE
            arrays = (["P0"], ["I"] if together else ["I", "O"], ["N1", "F2"], ["N2", "F3"])[g]
        if g == 0 and "E1" in WHOLE and "M1" in WHOLE:
            return Part(p, [self.reflectors], [(lambda z: z * wide, 0, wide)])
        found = []
        for name in arrays:
            got = self(name)
            found += got if isinstance(got, list) else [got]
        blocks = [(lambda z: places[g](z) * wide, 0, wide)]
        return Part(p, found, blocks, inner if len(found) > 1 else None)


def swap_sum(mine, other, m):
    mine = (mine.astype(F32) + swap(other, 1, m).astype(F32)).astype(BF16)
    bit = 2
    while bit < m:
        got = [swap(mine, s * bit, m) for s in range(1, 4) if s * bit < m]
        mine = sum([g.astype(F32) for g in got], mine.astype(F32)).astype(BF16)
        bit *= 4
    return mine, swap(mine, 1, m)


def plain_body(n, m, eigvecs, reflectors, factors):
    current = eigvecs
    for p in (1, 0):
        panel = lax.all_gather(reflectors[p], "vecs", axis=1, tiled=True)
        mine, other = jnp.split(dot(current, panel, 0, 0).astype(BF16), 2)
        odd = lax.axis_index("rows") % 2 == 1
        mine, other = swap_sum(jnp.where(odd, other, mine), jnp.where(odd, mine, other), m)
        total = jnp.where(odd, jnp.concatenate([other, mine]), jnp.concatenate([mine, other]))
        scaled = dot(factors[p], total, 1, 1).astype(BF16)
        current = (current.astype(F32) - dot(panel, scaled, 1, 0)).astype(BF16)
    return current


def solution(mesh):
    n, m = mesh.shape["vecs"], mesh.shape["rows"]

    def local(eigvecs, reflectors, factors):
        wide, columns, size = reflectors.shape[2], eigvecs.shape[1], factors.shape[1]
        fits = n == 4 and wide % 128 == 0 and columns % 32 == 0 and size % 256 == 0
        if fits:
            return Steps(n, m, eigvecs, reflectors, factors)("U0")
        return plain_body(n, m, eigvecs, reflectors, factors)

    in_specs = (P("rows", "vecs"), P(None, "rows", "vecs"), P())
    out_specs = P("rows", "vecs")
    return jax.shard_map(local, mesh=mesh, in_specs=in_specs, out_specs=out_specs, check_vma=False)
```

```python
import functools

import jax
import jax.numpy as jnp
from jax import lax
from jax.experimental import pallas as pl
from jax.experimental.pallas import tpu as pltpu
from jax.sharding import PartitionSpec as P

F32, BF16 = jnp.float32, jnp.bfloat16
VMEM = 16 << 20
ANY = pl.BlockSpec(memory_space=pl.ANY)
IN_VMEM = pl.BlockSpec(memory_space=pltpu.VMEM)


def after(x, *others):
    return lax.optimization_barrier((x,) + others)[0]


def held(*xs):
    return [x for x in xs if x is not None]


def dot(a, b, ca, cb):
    return lax.dot_general(a, b, (((ca,), (cb,)), ((), ())), preferred_element_type=F32)


def swap(x, bit, m):
    return lax.ppermute(x, "rows", [(i, i ^ bit) for i in range(m)])


class Part:
    def __init__(self, p, arrays, blocks, here=None):
        self.arrays, self.blocks, self.here = arrays, blocks, here
        self.leads = [p if x.ndim == 3 else None for x in arrays]
        self.rows, self.width = [x.shape[-2] for x in arrays], arrays[0].shape[-1]


def start_parts(parts, refs, panels, sems):
    waits, at, column = [], 0, 0
    for k, part in enumerate(parts):
        columns = pl.ds(column, part.width)
        own = [ref if p is None else ref.at[p] for ref, p in zip(refs[at : at + len(part.rows)], part.leads)]
        whole = pltpu.make_async_copy(own[0], panels.at[:, columns], sems.at[k])
        if part.here is None:
            whole.start()
        else:
            here = part.here(lax.axis_index("vecs"))
            pl.when(here)(whole.start)
            row = 0
            for i, rows in enumerate(part.rows[1:]):
                place = panels.at[pl.ds(row, rows), columns]
                piece = pltpu.make_async_copy(own[1 + i], place, sems.at[k])
                pl.when(jnp.logical_not(here))(piece.start)
                row += rows
        waits.append(whole.wait)
        at += len(part.rows)
        column += part.width
    return waits


def coeff_kernel(parts, current_ref, *refs):
    n = sum(len(part.rows) for part in parts)
    mine_ref, other_ref, current, panels, sems = refs[n:]
    copy = pltpu.make_async_copy(current_ref, current, sems.at[len(parts)])
    copy.start()
    waits = start_parts(parts, refs[:n], panels, sems)
    copy.wait()
    half = current.shape[0] // 2
    odd = lax.axis_index("rows") % 2 == 1
    column = 0
    for part, wait in zip(parts, waits):
        wait()
        at = slice(column, column + part.width)
        total = dot(current[...], panels[:, at], 1, 0)
        mine_ref[:, at] = jnp.where(odd, total[half:], total[:half]).astype(BF16)
        other_ref[:, at] = jnp.where(odd, total[:half], total[half:]).astype(BF16)
        column += part.width


class Copies:
    def __init__(self, sems):
        self.sems, self.count = sems, 0

    def __call__(self, source, target):
        copy = pltpu.make_async_copy(source, target, self.sems.at[self.count])
        self.count += 1
        copy.start()
        return copy.wait


def columns_at(place, width):
    return pl.ds(pl.multiple_of(place(lax.axis_index("vecs")), width), width)


def half_rows(whose, half):
    own = lax.axis_index("rows") % 2
    return pl.ds(pl.multiple_of(jnp.where(own == whose, 0, half), half), half)


def scale_kernel(p, groups, factors_ref, *refs):
    coeff_refs, (out_ref, factor, coeff, sems) = refs[: 2 * len(groups)], refs[2 * len(groups) :]
    size, half = factor.shape[0], coeff.shape[0] // 2
    copy = Copies(sems)
    tiles = []
    for t in reversed(range(0, size, 256)):
        rows, cols = pl.ds(t, 256), pl.ds(t, size - t)
        tiles.append((t, copy(factors_ref.at[p, rows, cols], factor.at[rows, cols])))
    coeff[...] = jnp.zeros_like(coeff)
    waits = []
    for k, ref in enumerate(coeff_refs):
        at = 0
        for part in groups[k // 2]:
            for place, offset, width in part.blocks:
                target = coeff.at[half_rows(k % 2, half), columns_at(place, width)]
                waits.append(copy(ref.at[:, pl.ds(at + offset, width)], target))
            at += part.width
    for wait in waits:
        wait()
    plain = coeff[...].T
    for t, wait in tiles:
        wait()
        out_ref[t : t + 256] = dot(factor[t : t + 256, t:], plain[t:], 1, 0).astype(BF16)


def prepare_kernel(p, last, parts, late, factors_ref, current_ref, scaled_ref, *refs):
    n = sum(len(part.rows) for part in parts)
    rest_ref, across_ref, current, met, panels, sems, panel_sems = refs[n:]
    columns = current.shape[0]
    copy = Copies(sems)
    parts_there = start_parts(parts, refs[:n], panels, panel_sems)
    waits = [copy(current_ref, current)]
    at = 0
    for part in parts:
        for place, offset, width in part.blocks:
            rows, there = pl.ds(at + offset, width), columns_at(place, width)
            waits.append(copy(scaled_ref.at[there], met.at[rows, pl.ds(0, columns)]))
            to = columns
            for other in late:
                for other_place, other_offset, other_width in other.blocks:
                    source = factors_ref.at[p, there, columns_at(other_place, other_width)]
                    waits.append(copy(source, met.at[rows, pl.ds(to + other_offset, other_width)]))
                to += other.width
        at += part.width
    for wait in waits + parts_there:
        wait()
    product = dot(panels[...], met[...], 1, 0)
    across_ref[...] = product[:, columns:].astype(BF16)
    if last:
        rest_ref[...] = current[...].astype(F32).T - product[:, :columns]
    else:
        rest_ref[...] = current[...].astype(F32) - product[:, :columns].T


def finish_kernel(last, rest_ref, across_ref, own_ref, other_ref, out_ref, rest, across, coeff, sems):
    copy = Copies(sems)
    half = coeff.shape[0] // 2
    waits = [copy(rest_ref, rest), copy(across_ref, across)]
    waits += [copy(ref, coeff.at[half_rows(k, half)]) for k, ref in enumerate((own_ref, other_ref))]
    for wait in waits:
        wait()
    product = dot(across[...], coeff[...], 1, 1) if last else dot(coeff[...], across[...], 1, 1)
    out_ref[...] = (rest[...] - product).astype(BF16)


def call(kernel, inputs, outs, scratch, flops):
    return pl.pallas_call(
        kernel,
        in_specs=[ANY] * len(inputs),
        out_specs=[IN_VMEM] * len(outs),
        out_shape=[jax.ShapeDtypeStruct(shape, dtype) for shape, dtype in outs],
        scratch_shapes=scratch,
        compiler_params=pltpu.CompilerParams(vmem_limit_bytes=VMEM),
        cost_estimate=pl.CostEstimate(
            flops=flops, bytes_accessed=sum(x.size * x.dtype.itemsize for x in inputs), transcendentals=0
        ),
    )(*inputs)


def arrays_of(parts):
    return [x for part in parts for x in part.arrays]


def scale(p, factors, groups, coeffs):
    size, columns = factors.shape[1], 2 * coeffs[0].shape[0]
    n_copies = size // 256 + 2 * sum(len(part.blocks) for group in groups for part in group)
    scratch = [
        pltpu.VMEM((size, size), BF16),
        pltpu.VMEM((columns, size), BF16),
        pltpu.SemaphoreType.DMA((n_copies,)),
    ]
    kernel = functools.partial(scale_kernel, p, groups)
    return call(kernel, [factors, *coeffs], [((size, columns), BF16)], scratch, size * size * columns)[0]


def prepare(p, last, factors, current, scaled, parts, late):
    columns, rows = current.shape
    size = factors.shape[1]
    more = sum(part.width for part in late)
    n_copies = 1 + sum(len(part.blocks) for part in parts) * (1 + sum(len(part.blocks) for part in late))
    scratch = [
        pltpu.VMEM((columns, rows), BF16),
        pltpu.VMEM((size, columns + more), BF16),
        pltpu.VMEM((rows, size), BF16),
        pltpu.SemaphoreType.DMA((n_copies,)),
        pltpu.SemaphoreType.DMA((len(parts),)),
    ]
    outs = [((rows, columns) if last else (columns, rows), F32), ((rows, more), BF16)]
    kernel = functools.partial(prepare_kernel, p, last, parts, late)
    inputs = [factors, current, scaled, *arrays_of(parts)]
    return call(kernel, inputs, outs, scratch, 2 * rows * size * (columns + more))


def finish(last, rest, across, coeffs):
    rows, more = across.shape
    columns = rest.size // rows
    scratch = [
        pltpu.VMEM(rest.shape, F32),
        pltpu.VMEM(across.shape, BF16),
        pltpu.VMEM((columns, more), BF16),
        pltpu.SemaphoreType.DMA((4,)),
    ]
    kernel = functools.partial(finish_kernel, last)
    return call(kernel, [rest, across, *coeffs], [(rest.shape, BF16)], scratch, 2 * rows * more * columns)[0]


def coeff(current, parts):
    columns, rows = current.shape
    size = sum(part.width for part in parts)
    arrays = [x for part in parts for x in part.arrays]
    return pl.pallas_call(
        functools.partial(coeff_kernel, parts),
        in_specs=[ANY] * (1 + len(arrays)),
        out_specs=[IN_VMEM] * 2,
        out_shape=[jax.ShapeDtypeStruct((columns // 2, size), BF16)] * 2,
        scratch_shapes=[
            pltpu.VMEM((columns, rows), BF16),
            pltpu.VMEM((rows, size), BF16),
            pltpu.SemaphoreType.DMA((len(parts) + 1,)),
        ],
        compiler_params=pltpu.CompilerParams(vmem_limit_bytes=VMEM),
        cost_estimate=pl.CostEstimate(
            flops=WEIGHT * 2 * size * columns * rows, bytes_accessed=WEIGHT * 2 * rows * size, transcendentals=0
        ),
    )(current, *arrays)


GROUPS = {1: ((0, 1), (2, 3)), 0: ((0, 1, 2), (3,))}
PIECES = {'O': 1, 'F3': 1}
JOINED = 'swap'
WHOLE = ()
WEIGHT = 16
DIRECT = ('0.0', '0.1', '0.2', '1.0', '1.1', '1.2')
SKIP = ('E3',)
GATES = {
    'X': ('p1',),
    'd1.0': ('I',),
    'a1.1': ('E3',),
    'c1.1': ('N2', 'F2', 'Y1'),
    'c0.1': ('Y0', 'F2'),
    'U1': ('N2',),
    'd0.1': ('N1',),
}


class Steps:
    def __init__(self, n, m, eigvecs, reflectors, factors):
        self.n, self.m, self.factors = n, m, factors
        self.eigvecs, self.reflectors = eigvecs, reflectors
        self.z = lax.axis_index("vecs")
        self.made = {}

    def __call__(self, name):
        if name not in self.made:
            self.made[name] = None
            self.made[name] = self.make(name)
        if self.made[name] is None:
            raise ValueError("circular gates")
        return self.made[name]

    def gated(self, name, x):
        others = []
        for other in GATES.get(name, ()):
            got = self(other)
            others += list(got) if isinstance(got, (tuple, list)) else [got]
        return after(x, *others) if others else x

    def send(self, name, x, pairs):
        return lax.ppermute(self.gated(name, x), "vecs", pairs)

    def pieces(self, name, x, pairs):
        size = x.shape[0] // PIECES[name]
        return [self.send(name, x[k * size : (k + 1) * size], pairs) for k in range(PIECES[name])]

    def make(self, name):
        n, z = self.n, self.z
        outer = [(i, i ^ 1) for i in range(n)]
        inward, outward = [(0, 1), (n - 1, n - 2)], [(1, 0), (n - 2, n - 1)]
        middle, skip = [(1, 2), (2, 1)], [(2, 0), (n - 3, n - 1)]
        at_end = (z == 0) | (z == n - 1)
        if name == "p1":
            return self.reflectors[1]
        if name == "P0":
            return self.gated(name, self.reflectors)[0]
        if name == "X":
            return self.gated(name, self.eigvecs).T
        if name in WHOLE:
            source = self.reflectors if name[1] == "1" else self({"E2": "M1", "M2": "E1"}[name])
            return self.send(name, source, middle if name[0] == "M" else outer if name == "E1" else outward)
        if name in ("E1", "M1", "E2", "M2", "E3"):
            if name in SKIP:
                return self.send(name, self.panel(1, "E1"), skip)
            source = {"E1": "p1", "M1": "p1", "E2": "M1", "M2": "E1", "E3": "M2"}[name]
            if name == "E2" and JOINED == "E2":
                return self.send(name, jnp.where(at_end, self("P0"), self.panel(1, "M1")), outer)
            return self.send(name, self.panel(1, source), {"E1": outer, "M1": middle, "M2": middle}.get(name, outward))
        twin = {"I": "E1", "N1": "M1", "F2": "E2", "N2": "M2"}.get(name)
        if twin in WHOLE:
            return self(twin)
        if name == "I":
            if JOINED == "E2":
                return self("E2")
            return self.send(name, self("P0"), outer if JOINED == "swap" else inward)
        if name == "O":
            return self.pieces(name, self("P0"), outward)
        if name in ("N1", "N2", "F2"):
            source = {"N1": "P0", "N2": "I", "F2": "N1"}[name]
            return self.send(name, self.panel(0, source), outward if name == "F2" else middle)
        if name == "F3":
            if name in SKIP:
                return self.pieces(name, self.panel(0, "I"), skip)
            return self.pieces(name, self.panel(0, "N2"), outward)
        step, p = name[0], int(name[1])
        groups = [[self.part(p, g) for g in group] for group in GROUPS[p]]
        late = len(groups) - 1
        if step == "S":
            coeffs = [self(f"{what}{p}.{k}") for k in range(late) for what in "cd"]
            return scale(p, self.gated(name, self.factors), groups[:late], coeffs)
        if step == "Y":
            current = self.gated(name, self("X" if p else "U1"))
            return prepare(p, p == 0, self.factors, current, self(f"S{p}"), sum(groups, []), groups[late])
        if step == "U":
            rest, across = self(f"Y{p}")
            coeffs = [self(f"{what}{p}.{late}") for what in "cd"]
            return finish(p == 0, self.gated(name, rest), across, coeffs)
        k = int(name[3:])
        if step == "a":
            return coeff(self.gated(name, self("U1" if p == 0 else "X")), groups[k])
        if step == "b":
            mine, other = self("a" + name[1:])
            got = self.gated(name, swap(other, 1, self.m))
            return (mine.astype(F32) + got.astype(F32)).astype(BF16)
        if step == "c":
            mine, bit = self("b" + name[1:]), 2
            while bit < self.m:
                if name[1:] in DIRECT or 2 * bit >= self.m:
                    got = [swap(mine, s * bit, self.m) for s in (3, 1, 2) if s * bit < self.m]
                    mine = sum([self.gated(name, g).astype(F32) for g in got], mine.astype(F32)).astype(BF16)
                else:
                    halves = jnp.split(mine, 2)
                    for bits in ((bit, 2 * bit), (2 * bit, bit)):
                        got = [swap(x, b, self.m) for x, b in zip(halves, bits)]
                        if bits[0] > bit:
                            got = [self.gated(name, g) for g in got]
                        halves = [(x.astype(F32) + g.astype(F32)).astype(BF16) for x, g in zip(halves, got)]
                    mine = jnp.concatenate(halves)
                bit *= 4
            return mine
        return swap(self.gated(name, self("c" + name[1:])), 1, self.m)

    def panel(self, p, name):
        x = self(name)
        return x[p] if x.ndim == 3 else x

    def part(self, p, g):
        n, wide = self.n, self.reflectors.shape[2]

        def inner(z):
            return (z > 0) & (z < n - 1)

        places = (
            lambda z: z,
            lambda z: z + 1 - 2 * (z % 2),
            lambda z: jnp.where(inner(z), n - 1 - z, (z + 2) % n),
            lambda z: jnp.where(inner(z), (z + 2) % n, n - 1 - z),
        )
        if p == 1:
            arrays = (["p1"], ["E1"], ["M1", "E2"], ["M2", "E3"])[g]
        else:
            together = JOINED == "swap" or "E1" in WHOLE
            arrays = (["P0"], ["I"] if together else ["I", "O"], ["N1", "F2"], ["N2", "F3"])[g]
        if g == 0 and "E1" in WHOLE and "M1" in WHOLE:
            return Part(p, [self.reflectors], [(lambda z: z * wide, 0, wide)])
        found = []
        for name in arrays:
            got = self(name)
            found += got if isinstance(got, list) else [got]
        blocks = [(lambda z: places[g](z) * wide, 0, wide)]
        return Part(p, found, blocks, inner if len(found) > 1 else None)


def swap_sum(mine, other, m):
    mine = (mine.astype(F32) + swap(other, 1, m).astype(F32)).astype(BF16)
    bit = 2
    while bit < m:
        got = [swap(mine, s * bit, m) for s in range(1, 4) if s * bit < m]
        mine = sum([g.astype(F32) for g in got], mine.astype(F32)).astype(BF16)
        bit *= 4
    return mine, swap(mine, 1, m)


def plain_body(n, m, eigvecs, reflectors, factors):
    current = eigvecs
    for p in (1, 0):
        panel = lax.all_gather(reflectors[p], "vecs", axis=1, tiled=True)
        mine, other = jnp.split(dot(current, panel, 0, 0).astype(BF16), 2)
        odd = lax.axis_index("rows") % 2 == 1
        mine, other = swap_sum(jnp.where(odd, other, mine), jnp.where(odd, mine, other), m)
        total = jnp.where(odd, jnp.concatenate([other, mine]), jnp.concatenate([mine, other]))
        scaled = dot(factors[p], total, 1, 1).astype(BF16)
        current = (current.astype(F32) - dot(panel, scaled, 1, 0)).astype(BF16)
    return current


def solution(mesh):
    n, m = mesh.shape["vecs"], mesh.shape["rows"]

    def local(eigvecs, reflectors, factors):
        wide, columns, size = reflectors.shape[2], eigvecs.shape[1], factors.shape[1]
        fits = n == 4 and wide % 128 == 0 and columns % 32 == 0 and size % 256 == 0
        if fits:
            return Steps(n, m, eigvecs, reflectors, factors)("U0")
        return plain_body(n, m, eigvecs, reflectors, factors)

    in_specs = (P("rows", "vecs"), P(None, "rows", "vecs"), P())
    out_specs = P("rows", "vecs")
    return jax.shard_map(local, mesh=mesh, in_specs=in_specs, out_specs=out_specs, check_vma=False)
```

```python
import functools

import jax
import jax.numpy as jnp
from jax import lax
from jax.experimental import pallas as pl
from jax.experimental.pallas import tpu as pltpu
from jax.sharding import PartitionSpec as P

F32, BF16 = jnp.float32, jnp.bfloat16
VMEM = 16 << 20
ANY = pl.BlockSpec(memory_space=pl.ANY)
IN_VMEM = pl.BlockSpec(memory_space=pltpu.VMEM)


def after(x, *others):
    return lax.optimization_barrier((x,) + others)[0]


def held(*xs):
    return [x for x in xs if x is not None]


def dot(a, b, ca, cb):
    return lax.dot_general(a, b, (((ca,), (cb,)), ((), ())), preferred_element_type=F32)


def swap(x, bit, m):
    return lax.ppermute(x, "rows", [(i, i ^ bit) for i in range(m)])


class Part:
    def __init__(self, p, arrays, blocks, here=None):
        self.arrays, self.blocks, self.here = arrays, blocks, here
        self.leads = [p if x.ndim == 3 else None for x in arrays]
        self.rows, self.width = [x.shape[-2] for x in arrays], arrays[0].shape[-1]


def start_parts(parts, refs, panels, sems):
    waits, at, column = [], 0, 0
    for k, part in enumerate(parts):
        columns = pl.ds(column, part.width)
        own = [ref if p is None else ref.at[p] for ref, p in zip(refs[at : at + len(part.rows)], part.leads)]
        whole = pltpu.make_async_copy(own[0], panels.at[:, columns], sems.at[k])
        if part.here is None:
            whole.start()
        else:
            here = part.here(lax.axis_index("vecs"))
            pl.when(here)(whole.start)
            row = 0
            for i, rows in enumerate(part.rows[1:]):
                place = panels.at[pl.ds(row, rows), columns]
                piece = pltpu.make_async_copy(own[1 + i], place, sems.at[k])
                pl.when(jnp.logical_not(here))(piece.start)
                row += rows
        waits.append(whole.wait)
        at += len(part.rows)
        column += part.width
    return waits


def coeff_kernel(parts, current_ref, *refs):
    n = sum(len(part.rows) for part in parts)
    mine_ref, other_ref, current, panels, sems = refs[n:]
    copy = pltpu.make_async_copy(current_ref, current, sems.at[len(parts)])
    copy.start()
    waits = start_parts(parts, refs[:n], panels, sems)
    copy.wait()
    half = current.shape[0] // 2
    odd = lax.axis_index("rows") % 2 == 1
    column = 0
    for part, wait in zip(parts, waits):
        wait()
        at = slice(column, column + part.width)
        total = dot(current[...], panels[:, at], 1, 0)
        mine_ref[:, at] = jnp.where(odd, total[half:], total[:half]).astype(BF16)
        other_ref[:, at] = jnp.where(odd, total[:half], total[half:]).astype(BF16)
        column += part.width


class Copies:
    def __init__(self, sems):
        self.sems, self.count = sems, 0

    def __call__(self, source, target):
        copy = pltpu.make_async_copy(source, target, self.sems.at[self.count])
        self.count += 1
        copy.start()
        return copy.wait


def columns_at(place, width):
    return pl.ds(pl.multiple_of(place(lax.axis_index("vecs")), width), width)


def half_rows(whose, half):
    own = lax.axis_index("rows") % 2
    return pl.ds(pl.multiple_of(jnp.where(own == whose, 0, half), half), half)


def scale_kernel(p, groups, factors_ref, *refs):
    coeff_refs, (out_ref, factor, coeff, sems) = refs[: 2 * len(groups)], refs[2 * len(groups) :]
    size, half = factor.shape[0], coeff.shape[0] // 2
    copy = Copies(sems)
    tiles = []
    for t in reversed(range(0, size, 256)):
        rows, cols = pl.ds(t, 256), pl.ds(t, size - t)
        tiles.append((t, copy(factors_ref.at[p, rows, cols], factor.at[rows, cols])))
    coeff[...] = jnp.zeros_like(coeff)
    waits = []
    for k, ref in enumerate(coeff_refs):
        at = 0
        for part in groups[k // 2]:
            for place, offset, width in part.blocks:
                target = coeff.at[half_rows(k % 2, half), columns_at(place, width)]
                waits.append(copy(ref.at[:, pl.ds(at + offset, width)], target))
            at += part.width
    for wait in waits:
        wait()
    plain = coeff[...].T
    for t, wait in tiles:
        wait()
        out_ref[t : t + 256] = dot(factor[t : t + 256, t:], plain[t:], 1, 0).astype(BF16)


def prepare_kernel(p, last, parts, late, factors_ref, current_ref, scaled_ref, *refs):
    n = sum(len(part.rows) for part in parts)
    rest_ref, across_ref, current, met, panels, sems, panel_sems = refs[n:]
    columns = current.shape[0]
    copy = Copies(sems)
    parts_there = start_parts(parts, refs[:n], panels, panel_sems)
    waits = [copy(current_ref, current)]
    at = 0
    for part in parts:
        for place, offset, width in part.blocks:
            rows, there = pl.ds(at + offset, width), columns_at(place, width)
            waits.append(copy(scaled_ref.at[there], met.at[rows, pl.ds(0, columns)]))
            to = columns
            for other in late:
                for other_place, other_offset, other_width in other.blocks:
                    source = factors_ref.at[p, there, columns_at(other_place, other_width)]
                    waits.append(copy(source, met.at[rows, pl.ds(to + other_offset, other_width)]))
                to += other.width
        at += part.width
    for wait in waits + parts_there:
        wait()
    product = dot(panels[...], met[...], 1, 0)
    across_ref[...] = product[:, columns:].astype(BF16)
    if last:
        rest_ref[...] = current[...].astype(F32).T - product[:, :columns]
    else:
        rest_ref[...] = current[...].astype(F32) - product[:, :columns].T


def finish_kernel(last, rest_ref, across_ref, own_ref, other_ref, out_ref, rest, across, coeff, sems):
    copy = Copies(sems)
    half = coeff.shape[0] // 2
    waits = [copy(rest_ref, rest), copy(across_ref, across)]
    waits += [copy(ref, coeff.at[half_rows(k, half)]) for k, ref in enumerate((own_ref, other_ref))]
    for wait in waits:
        wait()
    product = dot(across[...], coeff[...], 1, 1) if last else dot(coeff[...], across[...], 1, 1)
    out_ref[...] = (rest[...] - product).astype(BF16)


def call(kernel, inputs, outs, scratch, flops):
    return pl.pallas_call(
        kernel,
        in_specs=[ANY] * len(inputs),
        out_specs=[IN_VMEM] * len(outs),
        out_shape=[jax.ShapeDtypeStruct(shape, dtype) for shape, dtype in outs],
        scratch_shapes=scratch,
        compiler_params=pltpu.CompilerParams(vmem_limit_bytes=VMEM),
        cost_estimate=pl.CostEstimate(
            flops=flops, bytes_accessed=sum(x.size * x.dtype.itemsize for x in inputs), transcendentals=0
        ),
    )(*inputs)


def arrays_of(parts):
    return [x for part in parts for x in part.arrays]


def scale(p, factors, groups, coeffs):
    size, columns = factors.shape[1], 2 * coeffs[0].shape[0]
    n_copies = size // 256 + 2 * sum(len(part.blocks) for group in groups for part in group)
    scratch = [
        pltpu.VMEM((size, size), BF16),
        pltpu.VMEM((columns, size), BF16),
        pltpu.SemaphoreType.DMA((n_copies,)),
    ]
    kernel = functools.partial(scale_kernel, p, groups)
    return call(kernel, [factors, *coeffs], [((size, columns), BF16)], scratch, size * size * columns)[0]


def prepare(p, last, factors, current, scaled, parts, late):
    columns, rows = current.shape
    size = factors.shape[1]
    more = sum(part.width for part in late)
    n_copies = 1 + sum(len(part.blocks) for part in parts) * (1 + sum(len(part.blocks) for part in late))
    scratch = [
        pltpu.VMEM((columns, rows), BF16),
        pltpu.VMEM((size, columns + more), BF16),
        pltpu.VMEM((rows, size), BF16),
        pltpu.SemaphoreType.DMA((n_copies,)),
        pltpu.SemaphoreType.DMA((len(parts),)),
    ]
    outs = [((rows, columns) if last else (columns, rows), F32), ((rows, more), BF16)]
    kernel = functools.partial(prepare_kernel, p, last, parts, late)
    inputs = [factors, current, scaled, *arrays_of(parts)]
    return call(kernel, inputs, outs, scratch, 2 * rows * size * (columns + more))


def finish(last, rest, across, coeffs):
    rows, more = across.shape
    columns = rest.size // rows
    scratch = [
        pltpu.VMEM(rest.shape, F32),
        pltpu.VMEM(across.shape, BF16),
        pltpu.VMEM((columns, more), BF16),
        pltpu.SemaphoreType.DMA((4,)),
    ]
    kernel = functools.partial(finish_kernel, last)
    return call(kernel, [rest, across, *coeffs], [(rest.shape, BF16)], scratch, 2 * rows * more * columns)[0]


def coeff(current, parts, weight):
    columns, rows = current.shape
    size = sum(part.width for part in parts)
    arrays = [x for part in parts for x in part.arrays]
    return pl.pallas_call(
        functools.partial(coeff_kernel, parts),
        in_specs=[ANY] * (1 + len(arrays)),
        out_specs=[IN_VMEM] * 2,
        out_shape=[jax.ShapeDtypeStruct((columns // 2, size), BF16)] * 2,
        scratch_shapes=[
            pltpu.VMEM((columns, rows), BF16),
            pltpu.VMEM((rows, size), BF16),
            pltpu.SemaphoreType.DMA((len(parts) + 1,)),
        ],
        compiler_params=pltpu.CompilerParams(vmem_limit_bytes=VMEM),
        cost_estimate=pl.CostEstimate(
            flops=weight * 2 * size * columns * rows, bytes_accessed=weight * 2 * rows * size, transcendentals=0
        ),
    )(current, *arrays)


GROUPS = {1: ((0, 1), (2, 3)), 0: ((0, 1, 2), (3,))}
PIECES = {'O': 1, 'F3': 1}
JOINED = 'swap'
WHOLE = ()
WEIGHT = {'1.0': 64, '1.1': 1, '0.0': 16, '0.1': 16}
DIRECT = ('0.0', '0.1', '0.2', '1.0', '1.1', '1.2')
SKIP = ('E3',)
GATES = {
    'X': ('p1',),
    'd1.0': ('I',),
    'a1.1': ('E3',),
    'c1.1': ('N2', 'F2', 'Y1'),
    'c0.1': ('Y0', 'F2'),
    'U1': ('N2',),
    'd0.1': ('N1',),
}


class Steps:
    def __init__(self, n, m, eigvecs, reflectors, factors):
        self.n, self.m, self.factors = n, m, factors
        self.eigvecs, self.reflectors = eigvecs, reflectors
        self.z = lax.axis_index("vecs")
        self.made = {}

    def __call__(self, name):
        if name not in self.made:
            self.made[name] = None
            self.made[name] = self.make(name)
        if self.made[name] is None:
            raise ValueError("circular gates")
        return self.made[name]

    def gated(self, name, x):
        others = []
        for other in GATES.get(name, ()):
            got = self(other)
            others += list(got) if isinstance(got, (tuple, list)) else [got]
        return after(x, *others) if others else x

    def send(self, name, x, pairs):
        return lax.ppermute(self.gated(name, x), "vecs", pairs)

    def pieces(self, name, x, pairs):
        size = x.shape[0] // PIECES[name]
        return [self.send(name, x[k * size : (k + 1) * size], pairs) for k in range(PIECES[name])]

    def make(self, name):
        n, z = self.n, self.z
        outer = [(i, i ^ 1) for i in range(n)]
        inward, outward = [(0, 1), (n - 1, n - 2)], [(1, 0), (n - 2, n - 1)]
        middle, skip = [(1, 2), (2, 1)], [(2, 0), (n - 3, n - 1)]
        at_end = (z == 0) | (z == n - 1)
        if name == "p1":
            return self.reflectors[1]
        if name == "P0":
            return self.gated(name, self.reflectors)[0]
        if name == "X":
            return self.gated(name, self.eigvecs).T
        if name in WHOLE:
            source = self.reflectors if name[1] == "1" else self({"E2": "M1", "M2": "E1"}[name])
            return self.send(name, source, middle if name[0] == "M" else outer if name == "E1" else outward)
        if name in ("E1", "M1", "E2", "M2", "E3"):
            if name in SKIP:
                return self.send(name, self.panel(1, "E1"), skip)
            source = {"E1": "p1", "M1": "p1", "E2": "M1", "M2": "E1", "E3": "M2"}[name]
            if name == "E2" and JOINED == "E2":
                return self.send(name, jnp.where(at_end, self("P0"), self.panel(1, "M1")), outer)
            return self.send(name, self.panel(1, source), {"E1": outer, "M1": middle, "M2": middle}.get(name, outward))
        twin = {"I": "E1", "N1": "M1", "F2": "E2", "N2": "M2"}.get(name)
        if twin in WHOLE:
            return self(twin)
        if name == "I":
            if JOINED == "E2":
                return self("E2")
            return self.send(name, self("P0"), outer if JOINED == "swap" else inward)
        if name == "O":
            return self.pieces(name, self("P0"), outward)
        if name in ("N1", "N2", "F2"):
            source = {"N1": "P0", "N2": "I", "F2": "N1"}[name]
            return self.send(name, self.panel(0, source), outward if name == "F2" else middle)
        if name == "F3":
            if name in SKIP:
                return self.pieces(name, self.panel(0, "I"), skip)
            return self.pieces(name, self.panel(0, "N2"), outward)
        step, p = name[0], int(name[1])
        groups = [[self.part(p, g) for g in group] for group in GROUPS[p]]
        late = len(groups) - 1
        if step == "S":
            coeffs = [self(f"{what}{p}.{k}") for k in range(late) for what in "cd"]
            return scale(p, self.gated(name, self.factors), groups[:late], coeffs)
        if step == "Y":
            current = self.gated(name, self("X" if p else "U1"))
            return prepare(p, p == 0, self.factors, current, self(f"S{p}"), sum(groups, []), groups[late])
        if step == "U":
            rest, across = self(f"Y{p}")
            coeffs = [self(f"{what}{p}.{late}") for what in "cd"]
            return finish(p == 0, self.gated(name, rest), across, coeffs)
        k = int(name[3:])
        if step == "a":
            return coeff(self.gated(name, self("U1" if p == 0 else "X")), groups[k], WEIGHT[name[1:]])
        if step == "b":
            mine, other = self("a" + name[1:])
            got = self.gated(name, swap(other, 1, self.m))
            return (mine.astype(F32) + got.astype(F32)).astype(BF16)
        if step == "c":
            mine, bit = self("b" + name[1:]), 2
            while bit < self.m:
                if name[1:] in DIRECT or 2 * bit >= self.m:
                    got = [swap(mine, s * bit, self.m) for s in (3, 1, 2) if s * bit < self.m]
                    mine = sum([self.gated(name, g).astype(F32) for g in got], mine.astype(F32)).astype(BF16)
                else:
                    halves = jnp.split(mine, 2)
                    for bits in ((bit, 2 * bit), (2 * bit, bit)):
                        got = [swap(x, b, self.m) for x, b in zip(halves, bits)]
                        if bits[0] > bit:
                            got = [self.gated(name, g) for g in got]
                        halves = [(x.astype(F32) + g.astype(F32)).astype(BF16) for x, g in zip(halves, got)]
                    mine = jnp.concatenate(halves)
                bit *= 4
            return mine
        return swap(self.gated(name, self("c" + name[1:])), 1, self.m)

    def panel(self, p, name):
        x = self(name)
        return x[p] if x.ndim == 3 else x

    def part(self, p, g):
        n, wide = self.n, self.reflectors.shape[2]

        def inner(z):
            return (z > 0) & (z < n - 1)

        places = (
            lambda z: z,
            lambda z: z + 1 - 2 * (z % 2),
            lambda z: jnp.where(inner(z), n - 1 - z, (z + 2) % n),
            lambda z: jnp.where(inner(z), (z + 2) % n, n - 1 - z),
        )
        if p == 1:
            arrays = (["p1"], ["E1"], ["M1", "E2"], ["M2", "E3"])[g]
        else:
            together = JOINED == "swap" or "E1" in WHOLE
            arrays = (["P0"], ["I"] if together else ["I", "O"], ["N1", "F2"], ["N2", "F3"])[g]
        if g == 0 and "E1" in WHOLE and "M1" in WHOLE:
            return Part(p, [self.reflectors], [(lambda z: z * wide, 0, wide)])
        found = []
        for name in arrays:
            got = self(name)
            found += got if isinstance(got, list) else [got]
        blocks = [(lambda z: places[g](z) * wide, 0, wide)]
        return Part(p, found, blocks, inner if len(found) > 1 else None)


def swap_sum(mine, other, m):
    mine = (mine.astype(F32) + swap(other, 1, m).astype(F32)).astype(BF16)
    bit = 2
    while bit < m:
        got = [swap(mine, s * bit, m) for s in range(1, 4) if s * bit < m]
        mine = sum([g.astype(F32) for g in got], mine.astype(F32)).astype(BF16)
        bit *= 4
    return mine, swap(mine, 1, m)


def plain_body(n, m, eigvecs, reflectors, factors):
    current = eigvecs
    for p in (1, 0):
        panel = lax.all_gather(reflectors[p], "vecs", axis=1, tiled=True)
        mine, other = jnp.split(dot(current, panel, 0, 0).astype(BF16), 2)
        odd = lax.axis_index("rows") % 2 == 1
        mine, other = swap_sum(jnp.where(odd, other, mine), jnp.where(odd, mine, other), m)
        total = jnp.where(odd, jnp.concatenate([other, mine]), jnp.concatenate([mine, other]))
        scaled = dot(factors[p], total, 1, 1).astype(BF16)
        current = (current.astype(F32) - dot(panel, scaled, 1, 0)).astype(BF16)
    return current


def solution(mesh):
    n, m = mesh.shape["vecs"], mesh.shape["rows"]

    def local(eigvecs, reflectors, factors):
        wide, columns, size = reflectors.shape[2], eigvecs.shape[1], factors.shape[1]
        fits = n == 4 and wide % 128 == 0 and columns % 32 == 0 and size % 256 == 0
        if fits:
            return Steps(n, m, eigvecs, reflectors, factors)("U0")
        return plain_body(n, m, eigvecs, reflectors, factors)

    in_specs = (P("rows", "vecs"), P(None, "rows", "vecs"), P())
    out_specs = P("rows", "vecs")
    return jax.shard_map(local, mesh=mesh, in_specs=in_specs, out_specs=out_specs, check_vma=False)
```
